32 devices in a mesh: story: 8 (over y, x, core), col: 4 (over z).
Axes of the slice: x: 2, y: 2, z: 4, core: 2. Of those that a mesh axis runs over, the one named last changes fastest.
Arguments:
- inv_factor: bfloat16 [8, 2048, 2048], P('story', 'col'), may hold values from -1 to 1.5, as said below
- coupling_above: bfloat16 [8, 2048, 2048], P('story', 'col'), may hold values from -0.0029296875 to 0.0029296875
- coupling_below: bfloat16 [8, 2048, 2048], P('story', 'col'), may hold values from -0.0029296875 to 0.0029296875
- interior_loads: bfloat16 [8, 64, 2048], P('story'), may hold values from -18 to 18
- separator_loads: float32 [8, 64, 2048], P('story', None, 'col'), may hold values from -6 to 6
- lateral_pattern: bfloat16 [8, 2048], P('story'), may hold values from -0.03125 to 0.03125
- drift_pairs: int32 [256, 2], replicated, may hold values from 0 to 8, as said below
Outputs:
- solved_interior: float32 [8, 64, 2048], P('story', None, 'col')
- reduced_loads: float32 [8, 64, 2048], P('story', None, 'col')
- separator_update: float32 [8, 2048, 2048], P('story', 'col')
- separator_coupling: float32 [8, 2048, 2048], P('story', 'col')
- drift: float32 [256, 64], replicated
The draws below stay inside these ranges and needn't reach their ends.
Inputs may be any that keep to these rules, and one draw needn't show every extreme that they name: `inv_factor`: each matrix is lower triangular with a positive diagonal. `drift_pairs`: every row has a_p < b_p; row 0 is (0, 8).
All inputs are finite; a program needn't handle non-finite values.
Results may differ from the reference program's by a relative error of at most 0.0035.
Values may be sent and summed in bfloat16 or wider, within the bound.
A program may use at most 128 MiB of HBM per device.

```python
import math
import jax
import jax.numpy as jnp
from jax import lax

B = 2048
NCASE = 64
NPAIR = 256
STORIES = 8


def draw_inv_factor(key, part):
    key = jax.random.fold_in(key, 11)
    first_key, second_key = jax.random.split(key)
    rows = lax.broadcasted_iota(jnp.int32, (1, B, B), 1)
    columns = lax.broadcasted_iota(jnp.int32, (1, B, B), 2)
    lower = jax.random.truncated_normal(first_key, -6.0, 6.0, (STORIES, B, B), jnp.float32)
    diagonal = jax.random.uniform(second_key, (STORIES, B, B), jnp.float32, 0.5, 1.5)
    value = jnp.where(columns < rows, lower / math.sqrt(B), jnp.where(columns == rows, diagonal, 0.0))
    return value.astype(jnp.bfloat16)


def draw_interior_loads(key, part):
    key = jax.random.fold_in(key, 13)
    height = lax.broadcasted_iota(jnp.float32, (STORIES, 1, 1), 0)
    rise = 1.0 + 2.0 * height / max(STORIES - 1, 1)
    base = jax.random.truncated_normal(key, -6.0, 6.0, (STORIES, NCASE, B), jnp.float32)
    value = base * rise
    return value.astype(jnp.bfloat16)


def draw_drift_pairs(key, part):
    key = jax.random.fold_in(key, 17)
    first_key, second_key = jax.random.split(key)
    first_draw = jax.random.randint(first_key, (NPAIR,), 0, STORIES, jnp.int32)
    second_draw = jax.random.randint(second_key, (NPAIR,), 0, STORIES, jnp.int32)
    first_story = jnp.minimum(first_draw, second_draw).at[0].set(0)
    end_story = (jnp.maximum(first_draw, second_draw) + 1).at[0].set(STORIES)
    return jnp.stack([first_story, end_story], 1).astype(jnp.int32)


def steps_of(own_key, extent, pieces, low, largest):
    def one(position, shards_of):
        draws = jax.random.uniform(jax.random.fold_in(jax.random.fold_in(own_key, 6), position), (shards_of,), jnp.float32, low / len(pieces), largest / len(pieces))
        return jnp.repeat(jnp.exp(draws), extent[position] // shards_of).reshape((-1,) + (1,) * (len(extent) - position - 1))

    factor_of = one(*pieces[0])
    for cut in pieces[1:]:
        factor_of = factor_of * one(*cut)
    return factor_of


def centred(stream_key, extent, spread, reach, shards=(), held_as=jnp.bfloat16):
    result = spread * jax.random.normal(stream_key, extent, jnp.float32)
    if shards:
        result = result * steps_of(stream_key, extent, shards, -0.22, 0.18)
    return jnp.clip(result, -reach, reach).astype(held_as)


def setup_inputs(seed: int = 0) -> dict:
    splits = jax.random.split(jax.random.key(seed), 8)
    inv_factor = draw_inv_factor(jax.random.fold_in(splits[7], 71), 0)
    coupling_above = centred(splits[1], (STORIES, B, B), (B * B) ** -0.5, 0.0029296875, ((0, 8), (1, 4)))
    coupling_below = centred(splits[2], (STORIES, B, B), (B * B) ** -0.5, 0.0029296875, ((0, 8), (1, 4)))
    interior_loads = draw_interior_loads(jax.random.fold_in(splits[7], 71), 0)
    separator_loads = centred(splits[4], (STORIES, NCASE, B), 1.0, 6.0, ((0, 8), (2, 4)), jnp.float32)
    lateral_pattern = centred(splits[5], (STORIES, B), (16 * B) ** -0.5, 0.03125, ((0, 8),))
    drift_pairs = draw_drift_pairs(jax.random.fold_in(splits[7], 71), 0)
    return dict(inv_factor=inv_factor, coupling_above=coupling_above, coupling_below=coupling_below, interior_loads=interior_loads, separator_loads=separator_loads, lateral_pattern=lateral_pattern, drift_pairs=drift_pairs)


def panel_step(operands):
    inverse, above, below, loads, pattern = operands
    factor_above = jnp.dot(above, inverse.T, preferred_element_type=jnp.float32).astype(jnp.bfloat16)
    factor_below = jnp.dot(below, inverse.T, preferred_element_type=jnp.float32).astype(jnp.bfloat16)
    solved = jnp.dot(loads, inverse.T, preferred_element_type=jnp.float32)
    pattern_solved = jnp.dot(inverse, pattern, preferred_element_type=jnp.float32)
    return factor_above, factor_below, solved, pattern_solved


def schur_step(operands):
    above, below, upper, solved_half, upper_solved, sep_loads = operands
    update = jnp.dot(above, above.T, preferred_element_type=jnp.float32) + jnp.dot(upper, upper.T, preferred_element_type=jnp.float32)
    coupling = -jnp.dot(above, below.T, preferred_element_type=jnp.float32)
    reduced = sep_loads - jnp.dot(solved_half, above.T, preferred_element_type=jnp.float32) - jnp.dot(upper_solved, upper.T, preferred_element_type=jnp.float32)
    return update, coupling, reduced


def reference(inv_factor, coupling_above, coupling_below, interior_loads, separator_loads, lateral_pattern, drift_pairs):
    factor_above, factor_below, solved, pattern_solved = lax.map(panel_step, (inv_factor, coupling_above, coupling_below, interior_loads, lateral_pattern))
    solved_half = solved.astype(jnp.bfloat16)
    next_below = jnp.concatenate([factor_below[1:], jnp.zeros_like(factor_below[:1])], 0)
    next_solved = jnp.concatenate([solved_half[1:], jnp.zeros_like(solved_half[:1])], 0)
    update, coupling, reduced = lax.map(schur_step, (factor_above, factor_below, next_below, solved_half, next_solved, separator_loads))
    story_work = jnp.einsum("sck,sk->sc", solved, pattern_solved, precision=lax.Precision.HIGHEST)
    levels = jnp.arange(STORIES, dtype=jnp.int32)
    first_story = drift_pairs[:, 0]
    end_story = drift_pairs[:, 1]
    inside = ((levels[None, :] >= first_story[:, None]) & (levels[None, :] < end_story[:, None])).astype(jnp.float32)
    drift = jnp.dot(inside, story_work, precision=lax.Precision.HIGHEST)
    return solved, reduced, update, coupling, drift
```

```python
import jax
import jax.numpy as jnp
from jax import lax
from jax.sharding import PartitionSpec as P

BF16 = jnp.bfloat16
F32 = jnp.float32


def across(value, axis, pairs):
    return lax.ppermute(value, axis, pairs)


def from_above(value):
    count = lax.axis_size("story")
    return lax.ppermute(value, "story", [(j + 1, j) for j in range(count - 1)])


def transposed(first_operand, second_operand):
    return lax.dot_general(first_operand, second_operand, (((1,), (1,)), ((), ())), preferred_element_type=F32)


def drift_of(story_part, drift_pairs):
    stories = lax.axis_size("story")
    levels = jnp.arange(stories, dtype=jnp.int32)
    mine = (levels == lax.axis_index("story"))[:, None]
    work = lax.psum(jnp.where(mine, story_part[None, :], 0.0), ("story", "col"))
    first_story = drift_pairs[:, 0]
    end_story = drift_pairs[:, 1]
    inside = (levels[None, :] >= first_story[:, None]) & (levels[None, :] < end_story[:, None])
    return jnp.dot(inside.astype(F32), work, precision=lax.Precision.HIGHEST)


def gathered_form(inverse, above, below, loads, sep_loads):
    share = inverse.shape[0]
    operands = jnp.concatenate([above, below, loads], 0)
    panel = transposed(operands, lax.all_gather(inverse, "col", axis=0, tiled=True))
    factors = panel[: 2 * share].astype(BF16)
    factor_above, factor_below = factors[:share], factors[share:]
    solved_half = panel[2 * share :].astype(BF16)
    whole = lax.all_gather(jnp.stack([factor_above, factor_below]), "col", axis=1, tiled=True)
    square_below = transposed(factor_below, whole[1]).astype(BF16)
    loads_below = transposed(solved_half, factor_below)
    next_square, next_loads = from_above((square_below, loads_below))
    update = transposed(factor_above, whole[0]) + next_square.astype(F32)
    coupling = -transposed(factor_above, whole[1])
    reduced = sep_loads - transposed(solved_half, factor_above) - next_loads
    return reduced, update, coupling


def middle_form(inverse, above, below, loads, sep_loads):
    share = inverse.shape[0]
    half = share // 2
    width = 4 * share
    col = lax.axis_index("col")
    right = col == 2

    def widened(value):
        return jnp.pad(value, ((0, 0), (0, width - value.shape[1])))

    inv_1to2 = across(inverse[:, : 2 * share], "col", [(1, 2)])
    inv_0to1 = across(inverse[:, :share], "col", [(0, 1)])
    inv_0to2 = across(inverse[:, :share], "col", [(0, 2)])
    inv_3to2 = across(inverse, "col", [(3, 2)])
    inv_2to1 = across(inverse[:, : 3 * share], "col", [(2, 1)])
    inv_3to1 = across(inv_3to2, "col", [(2, 1)])

    def chunk(part):
        rows = slice(part * half, (part + 1) * half)
        return jnp.concatenate([above[rows], below[rows]], 0)

    own_c = [chunk(0), chunk(1)]
    end_c = [across(piece, "col", [(0, 1), (3, 2)]) for piece in own_c]
    om_c = [across(piece, "col", [(1, 2)]) for piece in own_c]
    oe_c = []
    for piece, before in zip(end_c, om_c):
        piece, _ = lax.optimization_barrier((piece, before))
        oe_c.append(across(piece, "col", [(1, 2)]))

    inv_end = widened(inv_0to1) + inv_3to2
    inv_om = widened(inv_1to2) + widened(inv_2to1)
    inv_oe = widened(inv_0to2) + inv_3to1
    inv_all = jnp.concatenate([inverse, inv_end, inv_om, inv_oe], 0)

    solved_half = transposed(loads, inv_all).astype(BF16)
    solved_two = jnp.concatenate([solved_half, from_above(solved_half)], 1)

    def factored(pieces):
        product = [transposed(piece, inv_all).astype(BF16) for piece in pieces]
        a = jnp.concatenate([piece[:half] for piece in product], 0)
        b = jnp.concatenate([piece[half:] for piece in product], 0)
        return a, b, jnp.concatenate([a, from_above(b)], 1)

    a_own, b_own, w_own = factored(own_c)
    a_end, b_end, w_end = factored(end_c)
    b_near = jnp.concatenate([b_own, b_end], 0)
    w_near = jnp.concatenate([w_own, w_end], 0)

    up_own_near = transposed(w_own, w_near)
    cp_own_near = -transposed(a_own, b_near)
    up_end_near = transposed(w_end, w_near).astype(BF16)
    cp_end_near = (-transposed(a_end, b_near)).astype(BF16)
    near_pair = across(jnp.stack([up_end_near, cp_end_near]), "col", [(1, 0), (2, 3)])
    taken_own = transposed(solved_two, w_own)
    taken_end = across(transposed(solved_two, w_end), "col", [(1, 0), (2, 3)])

    a_om, b_om, w_om = factored(om_c)
    om_back = across(
        jnp.stack([transposed(w_om, w_near).astype(BF16), (-transposed(a_om, b_near)).astype(BF16)]), "col", [(2, 1)]
    )
    om_out = across(
        jnp.stack([transposed(w_end, w_om).astype(BF16), (-transposed(a_end, b_om)).astype(BF16)]), "col", [(2, 3)]
    )
    up_own_om, cp_own_om = transposed(w_own, w_om), -transposed(a_own, b_om)

    oe_back, oe_out, up_own_oe, cp_own_oe = [], [], [], []
    for piece in oe_c:
        a_oe, b_oe, w_oe = factored([piece])
        oe_back.append(
            across(
                jnp.stack([transposed(w_oe, w_near).astype(BF16), (-transposed(a_oe, b_near)).astype(BF16)]),
                "col",
                [(2, 0)],
            )
        )
        oe_out.append(
            across(
                jnp.stack([transposed(w_end, w_oe).astype(BF16), (-transposed(a_end, b_oe)).astype(BF16)]),
                "col",
                [(2, 3)],
            )
        )
        up_own_oe.append(transposed(w_own, w_oe))
        cp_own_oe.append(-transposed(a_own, b_oe))
    oe_back = jnp.concatenate(oe_back, 1)

    def assembled(which, own_near, own_om, own_oe):
        near = near_pair[which].astype(F32)
        swap = lambda pair: jnp.concatenate([pair[:, share:], pair[:, :share]], 1)
        row_0 = jnp.concatenate([swap(near), oe_back[which].astype(F32)], 1)
        row_1 = jnp.concatenate([swap(own_near), om_back[which].astype(F32)], 1)
        row_2 = jnp.concatenate([*own_oe, own_om, own_near], 1)
        row_3 = jnp.concatenate(
            [*[piece[which].astype(F32) for piece in oe_out], om_out[which].astype(F32), near], 1
        )
        low = jnp.where(col == 0, row_0, row_1)
        high = jnp.where(right, row_2, row_3)
        return jnp.where(col < 2, low, high)

    update = assembled(0, up_own_near, up_own_om, up_own_oe)
    coupling = assembled(1, cp_own_near, cp_own_om, cp_own_oe)
    middle = (col == 1) | right
    reduced = sep_loads - jnp.where(middle, taken_own, taken_end)
    return reduced, update, coupling


def per_device(
    inv_factor,
    coupling_above,
    coupling_below,
    interior_loads,
    separator_loads,
    lateral_pattern,
    drift_pairs,
):
    inverse = inv_factor[0]
    loads = interior_loads[0]
    solved_rows = transposed(loads, inverse)
    pattern_rows = jnp.dot(inverse, lateral_pattern[0], preferred_element_type=F32)
    story_part = jnp.dot(solved_rows, pattern_rows, precision=lax.Precision.HIGHEST)
    form = middle_form if lax.axis_size("col") == 4 else gathered_form
    reduced, update, coupling = form(inverse, coupling_above[0], coupling_below[0], loads, separator_loads[0])
    drift = drift_of(story_part, drift_pairs)
    return (solved_rows[None], reduced[None], update[None], coupling[None], drift)


def solution(mesh):
    placed = (
        P("story", "col", None),
        P("story", "col", None),
        P("story", "col", None),
        P("story", None, None),
        P("story", None, "col"),
        P("story", None),
        P(),
    )
    return jax.shard_map(
        per_device,
        mesh=mesh,
        in_specs=placed,
        out_specs=(
            P("story", None, "col"),
            P("story", None, "col"),
            P("story", "col", None),
            P("story", "col", None),
            P(),
        ),
        check_vma=False,
    )
```

```python
import jax
import jax.numpy as jnp
from jax import lax
from jax.sharding import PartitionSpec as P

BF16 = jnp.bfloat16
F32 = jnp.float32


def across(value, axis, pairs):
    return lax.ppermute(value, axis, pairs)


def from_above(value):
    count = lax.axis_size("story")
    return lax.ppermute(value, "story", [(j + 1, j) for j in range(count - 1)])


def transposed(first_operand, second_operand):
    return lax.dot_general(first_operand, second_operand, (((1,), (1,)), ((), ())), preferred_element_type=F32)


def summed(value, axis):
    count = lax.axis_size(axis)
    if count & (count - 1):
        return lax.psum(value, axis)
    step = 1
    while step < count:
        value = value + lax.ppermute(value, axis, [(i, i ^ step) for i in range(count)])
        step *= 2
    return value


def drift_of(story_part, drift_pairs):
    stories = lax.axis_size("story")
    levels = jnp.arange(stories, dtype=jnp.int32)
    mine = (levels == lax.axis_index("story"))[:, None]
    work = summed(summed(jnp.where(mine, story_part[None, :], 0.0), "col"), "story")
    first_story = drift_pairs[:, 0]
    end_story = drift_pairs[:, 1]
    inside = (levels[None, :] >= first_story[:, None]) & (levels[None, :] < end_story[:, None])
    return jnp.dot(inside.astype(F32), work, precision=lax.Precision.HIGHEST)


def gathered_form(inverse, above, below, loads, sep_loads):
    share = inverse.shape[0]
    operands = jnp.concatenate([above, below, loads], 0)
    panel = transposed(operands, lax.all_gather(inverse, "col", axis=0, tiled=True))
    factors = panel[: 2 * share].astype(BF16)
    factor_above, factor_below = factors[:share], factors[share:]
    solved_half = panel[2 * share :].astype(BF16)
    whole = lax.all_gather(jnp.stack([factor_above, factor_below]), "col", axis=1, tiled=True)
    square_below = transposed(factor_below, whole[1]).astype(BF16)
    loads_below = transposed(solved_half, factor_below)
    next_square, next_loads = from_above((square_below, loads_below))
    update = transposed(factor_above, whole[0]) + next_square.astype(F32)
    coupling = -transposed(factor_above, whole[1])
    reduced = sep_loads - transposed(solved_half, factor_above) - next_loads
    return reduced, update, coupling


def middle_form(inverse, above, below, loads, sep_loads):
    share = inverse.shape[0]
    width = 4 * share
    col = lax.axis_index("col")
    right = col == 2
    to_middle = [(0, 1), (3, 2)]
    to_ends = [(1, 0), (2, 3)]

    inv_end = across(inverse, "col", to_middle)
    inv_om = across(inverse[:, : 3 * share], "col", [(1, 2), (2, 1)])
    inv_0to2 = across(inverse[:, :share], "col", [(0, 2)])
    below_end = across(below, "col", to_middle)
    below_om = across(below, "col", [(1, 2)])
    inv_3to1 = across(inv_end, "col", [(2, 1)])
    above_end = across(above, "col", to_middle)
    above_om = across(above, "col", [(1, 2)])
    below_oe, _ = lax.optimization_barrier((below_end, below_om))
    below_oe = across(below_oe, "col", [(1, 2)])
    above_oe, _ = lax.optimization_barrier((above_end, above_om))
    above_oe = across(above_oe, "col", [(1, 2)])

    inv_oe = jnp.pad(inv_0to2, ((0, 0), (0, width - share))) + inv_3to1
    inv_all = jnp.zeros((width, width), BF16)
    for place, rows in enumerate((inverse, inv_end, inv_om, inv_oe)):
        inv_all = lax.dynamic_update_slice(inv_all, rows, (place * share, 0))
    inv_all = lax.optimization_barrier(inv_all)

    def factored(rows):
        return lax.optimization_barrier(transposed(rows, inv_all).astype(BF16))

    b_own = factored(below)
    n_own = from_above(b_own)
    b_end = factored(below_end)
    n_end = from_above(b_end)
    solved_half = transposed(loads, inv_all).astype(BF16)
    next_half = from_above(solved_half)
    a_own = factored(above)
    a_end = factored(above_end)
    b_om = factored(below_om)
    n_om = from_above(b_om)
    a_om = factored(above_om)
    b_oe = factored(below_oe)
    n_oe = from_above(b_oe)
    a_oe = factored(above_oe)

    def update_of(first, second):
        return transposed(first[0], second[0]) + transposed(first[1], second[1])

    def sent(values, pairs):
        return [across(value.astype(BF16), "col", pairs).astype(F32) for value in values]

    own, end, om, oe = (a_own, n_own), (a_end, n_end), (a_om, n_om), (a_oe, n_oe)

    def returned(rows, columns, pairs):
        up = [update_of(rows[:2], column[:2]) for column in columns]
        cp = [-transposed(rows[0], column[2]) for column in columns]
        return sent(up, pairs), sent(cp, pairs)

    own, end, om, oe = own + (b_own,), end + (b_end,), om + (b_om,), oe + (b_oe,)
    near_up, near_cp = returned(end, (end, own), to_ends)
    taken_end = across(transposed(solved_half, a_end) + transposed(next_half, n_end), "col", to_ends)
    taken_own = transposed(solved_half, a_own) + transposed(next_half, n_own)
    back_om = returned(om, (own, end), [(2, 1)])
    out_om = returned(end, (om,), [(2, 3)])
    back_oe = returned(oe, (own, end), [(2, 0)])
    out_oe = returned(end, (oe,), [(2, 3)])
    mine_up = [update_of(own[:2], column[:2]) for column in (end, own, om, oe)]
    mine_cp = [-transposed(a_own, column) for column in (b_end, b_own, b_om, b_oe)]

    def assembled(which, near, mine):
        rows = (
            (near[0], near[1], back_oe[which][0], back_oe[which][1]),
            (mine[0], mine[1], back_om[which][0], back_om[which][1]),
            (mine[3], mine[2], mine[1], mine[0]),
            (out_oe[which][0], out_om[which][0], near[1], near[0]),
        )
        blocks = []
        for at in range(4):
            low = jnp.where(col == 0, rows[0][at], rows[1][at])
            high = jnp.where(right, rows[2][at], rows[3][at])
            blocks.append(jnp.where(col < 2, low, high))
        return jnp.concatenate(blocks, 1)

    update = assembled(0, near_up, mine_up)
    coupling = assembled(1, near_cp, mine_cp)
    reduced = sep_loads - jnp.where((col == 1) | right, taken_own, taken_end)
    return reduced, update, coupling


def per_device(
    inv_factor,
    coupling_above,
    coupling_below,
    interior_loads,
    separator_loads,
    lateral_pattern,
    drift_pairs,
):
    inverse = inv_factor[0]
    loads = interior_loads[0]
    solved_rows = transposed(loads, inverse)
    pattern_rows = jnp.dot(inverse, lateral_pattern[0], preferred_element_type=F32)
    story_part = jnp.dot(solved_rows, pattern_rows, precision=lax.Precision.HIGHEST)
    form = middle_form if lax.axis_size("col") == 4 else gathered_form
    reduced, update, coupling = form(inverse, coupling_above[0], coupling_below[0], loads, separator_loads[0])
    drift = drift_of(story_part, drift_pairs)
    return (solved_rows[None], reduced[None], update[None], coupling[None], drift)


def solution(mesh):
    placed = (
        P("story", "col", None),
        P("story", "col", None),
        P("story", "col", None),
        P("story", None, None),
        P("story", None, "col"),
        P("story", None),
        P(),
    )
    return jax.shard_map(
        per_device,
        mesh=mesh,
        in_specs=placed,
        out_specs=(
            P("story", None, "col"),
            P("story", None, "col"),
            P("story", "col", None),
            P("story", "col", None),
            P(),
        ),
        check_vma=False,
    )
```

```python
import jax
import jax.numpy as jnp
from jax import lax
from jax.sharding import PartitionSpec as P

BF16 = jnp.bfloat16
F32 = jnp.float32


def across(value, axis, pairs):
    return lax.ppermute(value, axis, pairs)


def from_above(value):
    count = lax.axis_size("story")
    return lax.ppermute(value, "story", [(j + 1, j) for j in range(count - 1)])


def transposed(first_operand, second_operand):
    return lax.dot_general(first_operand, second_operand, (((1,), (1,)), ((), ())), preferred_element_type=F32)


def summed(value, axis):
    count = lax.axis_size(axis)
    if count & (count - 1):
        return lax.psum(value, axis)
    step = 1
    while step < count:
        value = value + lax.ppermute(value, axis, [(i, i ^ step) for i in range(count)])
        step *= 2
    return value


def drift_of(story_part, drift_pairs):
    stories = lax.axis_size("story")
    levels = jnp.arange(stories, dtype=jnp.int32)
    mine = (levels == lax.axis_index("story"))[:, None]
    work = summed(summed(jnp.where(mine, story_part[None, :], 0.0), "col"), "story")
    first_story = drift_pairs[:, 0]
    end_story = drift_pairs[:, 1]
    inside = (levels[None, :] >= first_story[:, None]) & (levels[None, :] < end_story[:, None])
    return jnp.dot(inside.astype(F32), work, precision=lax.Precision.HIGHEST)


def gathered_form(inverse, above, below, loads, sep_loads):
    share = inverse.shape[0]
    operands = jnp.concatenate([above, below, loads], 0)
    panel = transposed(operands, lax.all_gather(inverse, "col", axis=0, tiled=True))
    factors = panel[: 2 * share].astype(BF16)
    factor_above, factor_below = factors[:share], factors[share:]
    solved_half = panel[2 * share :].astype(BF16)
    whole = lax.all_gather(jnp.stack([factor_above, factor_below]), "col", axis=1, tiled=True)
    square_below = transposed(factor_below, whole[1]).astype(BF16)
    loads_below = transposed(solved_half, factor_below)
    next_square, next_loads = from_above((square_below, loads_below))
    update = transposed(factor_above, whole[0]) + next_square.astype(F32)
    coupling = -transposed(factor_above, whole[1])
    reduced = sep_loads - transposed(solved_half, factor_above) - next_loads
    return reduced, update, coupling, update


def middle_form(inverse, above, below, loads, sep_loads):
    share = inverse.shape[0]
    width = 4 * share
    col = lax.axis_index("col")
    right = col == 2
    to_middle = [(0, 1), (3, 2)]
    to_ends = [(1, 0), (2, 3)]

    inv_end = across(inverse, "col", to_middle)
    inv_om = across(inverse[:, : 3 * share], "col", [(1, 2), (2, 1)])
    inv_0to2 = across(inverse[:, :share], "col", [(0, 2)])
    below_end = across(below, "col", to_middle)
    below_om = across(below, "col", [(1, 2)])
    inv_3to1 = across(inv_end, "col", [(2, 1)])
    above_end = across(above, "col", to_middle)
    above_om = across(above, "col", [(1, 2)])
    below_oe, _ = lax.optimization_barrier((below_end, below_om))
    below_oe = across(below_oe, "col", [(1, 2)])
    above_oe, _ = lax.optimization_barrier((above_end, above_om))
    above_oe = across(above_oe, "col", [(1, 2)])

    inv_oe = jnp.pad(inv_0to2, ((0, 0), (0, width - share))) + inv_3to1
    inv_all = jnp.zeros((width, width), BF16)
    for place, rows in enumerate((inverse, inv_end, inv_om, inv_oe)):
        inv_all = lax.dynamic_update_slice(inv_all, rows, (place * share, 0))
    inv_all = lax.optimization_barrier(inv_all)

    def factored(rows):
        return lax.optimization_barrier(transposed(rows, inv_all).astype(BF16))

    def after(value, other):
        return lax.optimization_barrier((value, other))[0]

    b_own = factored(below)
    n_own = from_above(b_own)
    b_end = factored(after(below_end, b_own))
    n_end = from_above(b_end)
    b_om = factored(after(below_om, b_end))
    n_om = from_above(b_om)
    b_oe = factored(after(below_oe, b_om))
    n_oe = from_above(b_oe)
    a_own = factored(after(above, b_oe))
    solved_half = transposed(loads, inv_all).astype(BF16)
    next_half = from_above(solved_half)
    a_end = factored(after(above_end, n_own))
    a_om = factored(after(above_om, n_end))
    a_oe = factored(after(above_oe, n_om))

    def update_of(first, second):
        return transposed(first[0], second[0]) + transposed(first[1], second[1])

    def sent(values, pairs):
        return [across(value.astype(BF16), "col", pairs).astype(F32) for value in values]

    own, end, om, oe = (a_own, n_own), (a_end, n_end), (a_om, n_om), (a_oe, n_oe)

    def returned(rows, columns, pairs):
        up = [update_of(rows[:2], column[:2]) for column in columns]
        cp = [-transposed(rows[0], column[2]) for column in columns]
        return sent(up, pairs), sent(cp, pairs)

    own, end, om, oe = own + (b_own,), end + (b_end,), om + (b_om,), oe + (b_oe,)
    near_up, near_cp = returned(end, (end, own), to_ends)
    taken_end = across(transposed(solved_half, a_end) + transposed(next_half, n_end), "col", to_ends)
    taken_own = transposed(solved_half, a_own) + transposed(next_half, n_own)
    back_om = returned(om, (own, end), [(2, 1)])
    out_om = returned(end, (om,), [(2, 3)])
    back_oe = returned(oe, (own, end), [(2, 0)])
    out_oe = returned(end, (oe,), [(2, 3)])
    mine_up = [update_of(own[:2], column[:2]) for column in (end, own, om, oe)]
    mine_cp = [-transposed(a_own, column) for column in (b_end, b_own, b_om, b_oe)]

    def assembled(which, near, mine):
        rows = (
            (near[0], near[1], back_oe[which][0], back_oe[which][1]),
            (mine[0], mine[1], back_om[which][0], back_om[which][1]),
            (mine[3], mine[2], mine[1], mine[0]),
            (out_oe[which][0], out_om[which][0], near[1], near[0]),
        )
        blocks = []
        for at in range(4):
            low = jnp.where(col == 0, rows[0][at], rows[1][at])
            high = jnp.where(right, rows[2][at], rows[3][at])
            blocks.append(jnp.where(col < 2, low, high))
        return jnp.concatenate(blocks, 1)

    update = assembled(0, near_up, mine_up)
    coupling = assembled(1, near_cp, mine_cp)
    reduced = sep_loads - jnp.where((col == 1) | right, taken_own, taken_end)
    return reduced, update, coupling, b_oe


def per_device(
    inv_factor,
    coupling_above,
    coupling_below,
    interior_loads,
    separator_loads,
    lateral_pattern,
    drift_pairs,
):
    inverse = inv_factor[0]
    loads = interior_loads[0]
    solved_rows = transposed(loads, inverse)
    pattern_rows = jnp.dot(inverse, lateral_pattern[0], preferred_element_type=F32)
    story_part = jnp.dot(solved_rows, pattern_rows, precision=lax.Precision.HIGHEST)
    form = middle_form if lax.axis_size("col") == 4 else gathered_form
    reduced, update, coupling, settled = form(inverse, coupling_above[0], coupling_below[0], loads, separator_loads[0])
    story_part, _ = lax.optimization_barrier((story_part, settled))
    drift = drift_of(story_part, drift_pairs)
    return (solved_rows[None], reduced[None], update[None], coupling[None], drift)


def solution(mesh):
    placed = (
        P("story", "col", None),
        P("story", "col", None),
        P("story", "col", None),
        P("story", None, None),
        P("story", None, "col"),
        P("story", None),
        P(),
    )
    return jax.shard_map(
        per_device,
        mesh=mesh,
        in_specs=placed,
        out_specs=(
            P("story", None, "col"),
            P("story", None, "col"),
            P("story", "col", None),
            P("story", "col", None),
            P(),
        ),
        check_vma=False,
    )
```

```python
import jax
import jax.numpy as jnp
from jax import lax
from jax.sharding import PartitionSpec as P

BF16 = jnp.bfloat16
F32 = jnp.float32


def across(value, axis, pairs):
    return lax.ppermute(value, axis, pairs)


def from_above(value):
    count = lax.axis_size("story")
    return lax.ppermute(value, "story", [(j + 1, j) for j in range(count - 1)])


def transposed(first_operand, second_operand):
    return lax.dot_general(first_operand, second_operand, (((1,), (1,)), ((), ())), preferred_element_type=F32)


def summed(value, axis):
    count = lax.axis_size(axis)
    if count & (count - 1):
        return lax.psum(value, axis)
    step = 1
    while step < count:
        value = value + lax.ppermute(value, axis, [(i, i ^ step) for i in range(count)])
        step *= 2
    return value


def drift_of(story_part, drift_pairs):
    stories = lax.axis_size("story")
    levels = jnp.arange(stories, dtype=jnp.int32)
    mine = (levels == lax.axis_index("story"))[:, None]
    work = summed(summed(jnp.where(mine, story_part[None, :], 0.0), "col"), "story")
    first_story = drift_pairs[:, 0]
    end_story = drift_pairs[:, 1]
    inside = (levels[None, :] >= first_story[:, None]) & (levels[None, :] < end_story[:, None])
    return jnp.dot(inside.astype(F32), work, precision=lax.Precision.HIGHEST)


def gathered_form(inverse, above, below, loads, sep_loads):
    share = inverse.shape[0]
    operands = jnp.concatenate([above, below, loads], 0)
    panel = transposed(operands, lax.all_gather(inverse, "col", axis=0, tiled=True))
    factors = panel[: 2 * share].astype(BF16)
    factor_above, factor_below = factors[:share], factors[share:]
    solved_half = panel[2 * share :].astype(BF16)
    whole = lax.all_gather(jnp.stack([factor_above, factor_below]), "col", axis=1, tiled=True)
    square_below = transposed(factor_below, whole[1]).astype(BF16)
    loads_below = transposed(solved_half, factor_below)
    next_square, next_loads = from_above((square_below, loads_below))
    update = transposed(factor_above, whole[0]) + next_square.astype(F32)
    coupling = -transposed(factor_above, whole[1])
    reduced = sep_loads - transposed(solved_half, factor_above) - next_loads
    return reduced, update, coupling, update


def middle_form(inverse, above, below, loads, sep_loads):
    share = inverse.shape[0]
    width = 4 * share
    col = lax.axis_index("col")
    right = col == 2
    to_middle = [(0, 1), (3, 2)]
    to_ends = [(1, 0), (2, 3)]

    inv_end = across(inverse, "col", to_middle)
    inv_om = across(inverse[:, : 3 * share], "col", [(1, 2), (2, 1)])
    inv_0to2 = across(inverse[:, :share], "col", [(0, 2)])
    below_end = across(below, "col", to_middle)
    below_om = across(below, "col", [(1, 2)])
    inv_3to1 = across(inv_end, "col", [(2, 1)])
    above_later, _ = lax.optimization_barrier((above, (inv_om, inv_0to2)))
    above_end = across(above_later, "col", to_middle)
    above_om = across(above_later, "col", [(1, 2)])
    below_oe, _ = lax.optimization_barrier((below_end, below_om))
    below_oe = across(below_oe, "col", [(1, 2)])
    above_oe, _ = lax.optimization_barrier((above_end, above_om))
    above_oe = across(above_oe, "col", [(1, 2)])

    inv_oe = jnp.pad(inv_0to2, ((0, 0), (0, width - share))) + inv_3to1
    inv_all = jnp.zeros((width, width), BF16)
    for place, rows in enumerate((inverse, inv_end, inv_om, inv_oe)):
        inv_all = lax.dynamic_update_slice(inv_all, rows, (place * share, 0))
    inv_all = lax.optimization_barrier(inv_all)

    def factored(rows):
        return lax.optimization_barrier(transposed(rows, inv_all).astype(BF16))

    def after(value, other):
        return lax.optimization_barrier((value, other))[0]

    b_own = factored(below)
    n_own = from_above(b_own)
    b_end = factored(after(below_end, b_own))
    n_end = from_above(b_end)
    b_om = factored(after(below_om, b_end))
    n_om = from_above(b_om)
    b_oe = factored(after(below_oe, b_om))
    n_oe = from_above(b_oe)
    a_own = factored(after(above, b_oe))
    solved_half = transposed(loads, inv_all).astype(BF16)
    next_half = from_above(solved_half)
    a_end = factored(after(above_end, n_own))
    a_om = factored(after(above_om, n_end))
    a_oe = factored(after(above_oe, n_om))

    def update_of(first, second):
        return transposed(first[0], second[0]) + transposed(first[1], second[1])

    def sent(values, pairs):
        return [across(value.astype(BF16), "col", pairs).astype(F32) for value in values]

    own, end, om, oe = (a_own, n_own), (a_end, n_end), (a_om, n_om), (a_oe, n_oe)

    def returned(rows, columns, pairs):
        up = [update_of(rows[:2], column[:2]) for column in columns]
        cp = [-transposed(rows[0], column[2]) for column in columns]
        return sent(up, pairs), sent(cp, pairs)

    own, end, om, oe = own + (b_own,), end + (b_end,), om + (b_om,), oe + (b_oe,)
    near_up, near_cp = returned(end, (end, own), to_ends)
    taken_end = across(transposed(solved_half, a_end) + transposed(next_half, n_end), "col", to_ends)
    taken_own = transposed(solved_half, a_own) + transposed(next_half, n_own)
    back_om = returned(om, (own, end), [(2, 1)])
    out_om = returned(end, (om,), [(2, 3)])
    back_oe = returned(oe, (own, end), [(2, 0)])
    out_oe = returned(end, (oe,), [(2, 3)])
    mine_up = [update_of(own[:2], column[:2]) for column in (end, own, om, oe)]
    mine_cp = [-transposed(a_own, column) for column in (b_end, b_own, b_om, b_oe)]

    def assembled(which, near, mine):
        rows = (
            (near[0], near[1], back_oe[which][0], back_oe[which][1]),
            (mine[0], mine[1], back_om[which][0], back_om[which][1]),
            (mine[3], mine[2], mine[1], mine[0]),
            (out_oe[which][0], out_om[which][0], near[1], near[0]),
        )
        blocks = []
        for at in range(4):
            low = jnp.where(col == 0, rows[0][at], rows[1][at])
            high = jnp.where(right, rows[2][at], rows[3][at])
            blocks.append(jnp.where(col < 2, low, high))
        return jnp.concatenate(blocks, 1)

    update = assembled(0, near_up, mine_up)
    coupling = assembled(1, near_cp, mine_cp)
    reduced = sep_loads - jnp.where((col == 1) | right, taken_own, taken_end)
    return reduced, update, coupling, b_oe


def per_device(
    inv_factor,
    coupling_above,
    coupling_below,
    interior_loads,
    separator_loads,
    lateral_pattern,
    drift_pairs,
):
    inverse = inv_factor[0]
    loads = interior_loads[0]
    solved_rows = transposed(loads, inverse)
    pattern_rows = jnp.dot(inverse, lateral_pattern[0], preferred_element_type=F32)
    story_part = jnp.dot(solved_rows, pattern_rows, precision=lax.Precision.HIGHEST)
    form = middle_form if lax.axis_size("col") == 4 else gathered_form
    reduced, update, coupling, settled = form(inverse, coupling_above[0], coupling_below[0], loads, separator_loads[0])
    story_part, _ = lax.optimization_barrier((story_part, settled))
    drift = drift_of(story_part, drift_pairs)
    return (solved_rows[None], reduced[None], update[None], coupling[None], drift)


def solution(mesh):
    placed = (
        P("story", "col", None),
        P("story", "col", None),
        P("story", "col", None),
        P("story", None, None),
        P("story", None, "col"),
        P("story", None),
        P(),
    )
    return jax.shard_map(
        per_device,
        mesh=mesh,
        in_specs=placed,
        out_specs=(
            P("story", None, "col"),
            P("story", None, "col"),
            P("story", "col", None),
            P("story", "col", None),
            P(),
        ),
        check_vma=False,
    )
```
